32 devices in a mesh: dom: 8 (over z, x), row: 4 (over y, core).
Axes of the slice: x: 2, y: 2, z: 4, core: 2. Of those that a mesh axis runs over, the one named last changes fastest.
Arguments:
- right_side: float32 [8192, 128], P(('dom', 'row')), may hold values from -6 to 6
- spikes: float32 [3, 8192, 512], P(None, ('dom', 'row')), may hold values from -0.1875 to 0.1875
- inverses: float32 [8, 1024, 1024], P('dom', 'row'), may hold values from -1 to 2
Outputs:
- solution: float32 [8192, 128], P(('dom', 'row'))
The draws below stay inside these ranges and needn't reach their ends.
All inputs are finite; a program needn't handle non-finite values.
Results may differ from the reference program's by a relative error of at most 0.0001.
Values sent between devices are 32-bit elements; how exact they have to be, the bound alone decides.
A program may use at most 64 MiB of HBM per device.

```python
import math
import jax
import jax.numpy as jnp
from jax import lax

K = 512
NRHS = 128
PARTITIONS = 8
LEVELS = 3
ROWS = 8192


def draw_inverses(key, part):
    order = 2 * K
    spread_size = 0.5 / math.sqrt(order)
    bound_value = spread_size * math.sqrt(3.0)
    offsets = jax.random.uniform(key, (PARTITIONS, order, order), jnp.float32, -bound_value, bound_value)
    return offsets + jnp.eye(order, dtype=jnp.float32)[None]


def block_levels(own_key, extent, cuts, least, largest):
    gain = 1.0
    for position, blocks in cuts:
        heights = jax.random.uniform(jax.random.fold_in(jax.random.fold_in(own_key, 6), position), (blocks,), jnp.float32, least / len(cuts), largest / len(cuts))
        gain = gain * jnp.repeat(jnp.exp(heights), extent[position] // blocks).reshape((-1,) + (1,) * (len(extent) - 1 - position))
    return gain


def normal_values(key, shape, width, reach, pieces=(), kind=jnp.bfloat16):
    gain = block_levels(key, shape, pieces, -0.22, 0.18) if pieces else 1.0
    drawn = jax.random.normal(key, shape, jnp.float32) * width * gain
    return jnp.minimum(jnp.maximum(drawn, -reach), reach).astype(kind)


def setup_inputs(seed: int = 0) -> dict:
    arg_keys = jax.random.split(jax.random.key(seed), 4)
    return {
        "right_side": normal_values(arg_keys[0], (ROWS, NRHS), 1.0, 6.0, ((0, 32),), jnp.float32),
        "spikes": normal_values(arg_keys[1], (LEVELS, ROWS, K), (2 * K) ** -0.5, 0.1875, ((1, 32),), jnp.float32),
        "inverses": draw_inverses(jax.random.fold_in(arg_keys[3], 71), 0),
    }


exact_mode = lax.Precision.HIGHEST


def reference(right_side, spikes, inverses):
    total_rows, columns = right_side.shape
    spike_cols = spikes.shape[2]
    part_rows = total_rows // PARTITIONS
    current = right_side
    for level_at in range(LEVELS):
        half_group = 2 ** level_at
        block_rows = half_group * part_rows
        groups = PARTITIONS // (2 * half_group)
        shaped = current.reshape(groups, 2, block_rows, columns)
        tip_rows = jnp.concatenate([shaped[:, 0, block_rows - spike_cols:], shaped[:, 1, :spike_cols]], axis=1)
        owners = (jnp.arange(groups) * 2 * half_group + half_group).astype(jnp.int32)
        matrices = jnp.take(inverses, owners, axis=0)
        solved = jnp.einsum("gij,gjm->gim", matrices, tip_rows, precision=exact_mode)
        spike_rows = spikes[level_at].reshape(groups, 2, block_rows, spike_cols)
        left_term = jnp.einsum("gbk,gkm->gbm", spike_rows[:, 0], solved[:, spike_cols:], precision=exact_mode)
        right_term = jnp.einsum("gbk,gkm->gbm", spike_rows[:, 1], solved[:, :spike_cols], precision=exact_mode)
        shaped = shaped - jnp.stack([left_term, right_term], axis=1)
        current = shaped.reshape(total_rows, columns)
    return current
```

```python
import functools

import jax
import jax.numpy as jnp
from jax import lax
from jax.experimental import pallas as pl
from jax.experimental.pallas import tpu as pltpu
from jax.sharding import PartitionSpec as P

PARTS = 4


def split_pair(value):
    high = value.astype(jnp.bfloat16)
    low = (value - high.astype(jnp.float32)).astype(jnp.bfloat16)
    return high, low


def bf_dot(left, right):
    return jnp.dot(left, right, preferred_element_type=jnp.float32)


def kernel(
    row_count,
    right_ref,
    spikes_ref,
    inverse_ref,
    out_ref,
    right_buf,
    spike_buf,
    inverse_buf,
    inv_hi,
    inv_lo,
    spk_hi,
    spk_lo,
    cur,
    tips,
    piece,
    halves,
    last,
    local_sem,
    pair_send,
    pair_recv,
    a_send,
    a_recv,
    b_send,
    b_recv,
):
    levels, rows, depth = spikes_ref.shape
    columns = right_ref.shape[1]
    half_columns = columns // 2
    inv_rows = inverse_ref.shape[1]
    nodes = row_count // 2
    half_nodes = nodes // 2
    dom = lax.axis_index("dom")
    row = lax.axis_index("row")
    core = lax.rem(row, 2)
    node = row // 2
    other = 1 - core
    lane = lax.broadcasted_iota(jnp.int32, (1, columns), 1)

    def place(dom_at, node_at):
        return {"dom": dom_at, "row": 2 * node_at + core}

    sibling = {"dom": dom, "row": 2 * node + other}

    loads = [
        (right_ref, right_buf.at[core]),
        (inverse_ref.at[0], inverse_buf.at[core]),
    ] + [(spikes_ref.at[l], spike_buf.at[l, core]) for l in range(levels)]
    own, pair = [], []
    for index, (source, target) in enumerate(loads):
        send = pltpu.make_async_remote_copy(
            src_ref=source,
            dst_ref=target,
            send_sem=pair_send.at[index],
            recv_sem=pair_recv.at[index],
            device_id=sibling,
        )
        send.start()
        pair.append(send)
        copy = pltpu.make_async_copy(source, target, local_sem.at[index])
        copy.start()
        own.append(copy)

    def loaded(index):
        own[index].wait()
        pair[index].wait_recv()

    own_lanes = (lane < half_columns) == (core == 0)
    loaded(0)
    cur[0] = jnp.where(
        own_lanes, right_buf[core], pltpu.roll(right_buf[other], half_columns, 1)
    )

    def copy_to(source, target, send_sem, recv_sem, where):
        return pltpu.make_async_remote_copy(
            src_ref=source,
            dst_ref=target,
            send_sem=send_sem,
            recv_sem=recv_sem,
            device_id=where,
        )

    tip_chunk = rows // PARTS
    piece_chunk = inv_rows // PARTS
    tip_cut = [pl.ds(c * tip_chunk, tip_chunk) for c in range(PARTS)]
    piece_cut = [pl.ds(c * piece_chunk, piece_chunk) for c in range(PARTS)]
    waits = []

    def send_tips(source, slot, sem_at, c, where):
        copy_to(
            source.at[tip_cut[c]],
            tips.at[slot, tip_cut[c]],
            a_send.at[sem_at],
            a_recv.at[slot, c],
            where,
        ).start()

    def wait_tips(slot, c):
        copy_to(
            tips.at[slot, tip_cut[c]],
            tips.at[slot, tip_cut[c]],
            a_send.at[0],
            a_recv.at[slot, c],
            sibling,
        ).wait_recv()

    def packed(left, right):
        half = left.shape[0] // 2
        low = lane < half_columns
        straight = jnp.where(low, left[:half], right[half:])
        crossed = jnp.where(low, left[half:], right[:half])
        return straight + pltpu.roll(crossed, half_columns, 1)

    def product(hi_ref, lo_ref, messages):
        left = right = None
        for at, message in messages:
            high, low = split_pair(message)
            both = jnp.concatenate([high, low], axis=1)
            sums = []
            for side in range(2):
                cut = slice(at + side * rows, at + (side + 1) * rows)
                wide = bf_dot(hi_ref[:, cut], both)
                thin = bf_dot(lo_ref[:, cut], high)
                sums.append(wide[:, :columns] + (wide[:, columns:] + thin))
            left = sums[0] if left is None else left + sums[0]
            right = sums[1] if right is None else right + sums[1]
        return packed(left, right)

    def run_level(level):
        group = 1 << level
        offset = lax.rem(dom, 2 * group)
        base = dom - offset
        is_left = offset < group
        is_solver = offset == group
        solver_dom = base + group
        entry = max(group - 2, 0)
        from_bottom = (offset == group - 1) & (node == nodes - 1)

        @pl.when(from_bottom)
        def _():
            for c in range(PARTS):
                send_tips(cur.at[level], 0, 2 * nodes * level, c, place(dom + 1, nodes - 1))

        def across(step):
            return lax.rem(node + step, nodes)

        @pl.when(is_solver & (node == 0))
        def _():
            for c in range(PARTS):
                for step in range(1, nodes):
                    send_tips(cur.at[level], 1, 2 * nodes * level + step, c, place(dom, step))

        if level == 0:
            loaded(1)
            for side in range(2):
                high, low = split_pair(inverse_buf[side])
                at = slice(side * inv_rows, (side + 1) * inv_rows)
                inv_hi[at], inv_lo[at] = high, low

        relative = jnp.where(
            is_left, (offset // 2) * 2 + lax.rem(offset, 2) - entry, offset - group
        )
        if group >= 2:
            high_part = offset // 2
            flipped = (group // 2 - 1 - high_part) * 2 + lax.rem(offset, 2)
            relative = jnp.where(is_left, flipped, offset - group)
        else:
            relative = offset - offset
        piece_at = lax.rem(node, half_nodes)
        holder = jnp.where(is_left, node >= half_nodes, node < half_nodes)

        def spread(source, c, wait):
            def go(copy):
                copy.wait_send() if wait else copy.start()

            cut = piece_cut[c]
            target = halves.at[level, pl.ds(piece_at * inv_rows + c * piece_chunk, piece_chunk)]
            if wait:
                source, target = source, halves.at[level, pl.ds(piece_at * inv_rows, inv_rows)]
            else:
                source = source.at[cut]
            recv = b_recv.at[level, piece_at, c]
            bit, number = group // 2, 0
            while bit >= 1:
                child = relative + bit
                if group >= 2:
                    left_child = (group // 2 - 1 - child // 2) * 2 + lax.rem(child, 2)
                else:
                    left_child = child
                child_dom = base + jnp.where(is_left, left_child, group + child)

                @pl.when(lax.rem(relative, 2 * bit) == 0)
                def _(number=number, child_dom=child_dom):
                    go(copy_to(source, target, b_send.at[level, number], recv, place(child_dom, node)))

                bit //= 2
                number += 1
            for step in range(1, nodes):
                go(
                    copy_to(
                        source,
                        target,
                        b_send.at[level, levels + step],
                        recv,
                        place(dom, across(step)),
                    )
                )

        def to_left(c, wait):
            whole = pl.ds(piece_at * inv_rows, inv_rows)
            part = pl.ds(piece_at * inv_rows + c * piece_chunk, piece_chunk)
            copy = copy_to(
                piece if wait else piece.at[piece_cut[c]],
                halves.at[level, whole if wait else part],
                b_send.at[level, levels],
                b_recv.at[level, piece_at, c],
                place(base + entry, node),
            )
            copy.wait_send() if wait else copy.start()

        @pl.when(is_solver)
        def _():
            for c in range(PARTS):
                wait_tips(0, c)

                @pl.when(node == nodes - 1)
                def _():
                    for step in range(nodes - 1):
                        send_tips(
                            tips.at[0], 0, 2 * nodes * level + nodes + step, c, place(dom, step)
                        )

            @pl.when(node == 0)
            def _():
                tips[1] = cur[level]

            @pl.when(node != 0)
            def _():
                for c in range(PARTS):
                    wait_tips(1, c)

            piece[...] = product(inv_hi, inv_lo, [(0, tips[0]), (depth, tips[1])])

            @pl.when(node < half_nodes)
            def _():
                for c in range(PARTS):
                    spread(piece, c, False)
                halves[level, pl.ds(piece_at * inv_rows, inv_rows)] = piece[...]

            @pl.when(node >= half_nodes)
            def _():
                for c in range(PARTS):
                    to_left(c, False)

        loaded(2 + level)
        for side in range(2):
            high, low = split_pair(spike_buf[level, side])
            at = slice(side * rows, (side + 1) * rows)
            for value, target in ((high, spk_hi), (low, spk_lo)):
                if half_nodes > 1:
                    blocks = [
                        value[:, (2 * i + part) * inv_rows : (2 * i + part + 1) * inv_rows]
                        for part in range(2)
                        for i in range(half_nodes)
                    ]
                    value = jnp.concatenate(blocks, axis=1)
                target[level, at] = value

        for c in range(PARTS):
            for index in range(half_nodes):
                mine = is_solver & (node == index)
                forward = holder & (piece_at == index) & ~mine

                @pl.when(~mine)
                def _():
                    part = halves.at[level, pl.ds(index * inv_rows + c * piece_chunk, piece_chunk)]
                    copy_to(
                        part, part, b_send.at[0, 0], b_recv.at[level, index, c], sibling
                    ).wait_recv()

                @pl.when(forward)
                def _():
                    spread(halves.at[level, pl.ds(index * inv_rows, inv_rows)], c, False)

        update = product(spk_hi.at[level], spk_lo.at[level], [(0, halves[level])])
        cur[level + 1] = cur[level] - update

        def finish():
            @pl.when(from_bottom)
            def _():
                copy_to(
                    cur.at[level], tips.at[0], a_send.at[2 * nodes * level], a_recv.at[0, 0],
                    place(dom + 1, nodes - 1),
                ).wait_send()

            @pl.when(is_solver & (node == 0))
            def _():
                for step in range(1, nodes):
                    copy_to(
                        cur.at[level], tips.at[1], a_send.at[2 * nodes * level + step],
                        a_recv.at[1, 0], place(dom, step),
                    ).wait_send()

            @pl.when(is_solver & (node == nodes - 1))
            def _():
                for step in range(nodes - 1):
                    copy_to(
                        tips.at[0], tips.at[0], a_send.at[2 * nodes * level + nodes + step],
                        a_recv.at[0, 0], place(dom, step),
                    ).wait_send()

            @pl.when(is_solver & (node >= half_nodes))
            def _():
                to_left(0, True)

            @pl.when(holder)
            def _():
                spread(halves.at[level, pl.ds(piece_at * inv_rows, inv_rows)], 0, True)

        waits.append(finish)

    for level in range(levels):
        run_level(level)

    swap = copy_to(cur.at[levels], last, pair_send.at[levels + 2], pair_recv.at[levels + 2], sibling)
    swap.start()
    for finish in waits:
        finish()
    for send in pair:
        send.wait_send()
    swap.wait()
    out_ref[...] = jnp.where(own_lanes, cur[levels], pltpu.roll(last[...], half_columns, 1))


def body(right_side, spikes, inverses):
    row_count = lax.axis_size("row")
    rows, columns = right_side.shape
    levels, _, depth = spikes.shape
    inv_rows = inverses.shape[1]
    nodes = row_count // 2
    f32, bf16 = jnp.float32, jnp.bfloat16
    dma = pltpu.SemaphoreType.DMA
    return pl.pallas_call(
        functools.partial(kernel, row_count),
        out_shape=jax.ShapeDtypeStruct((rows, columns), f32),
        in_specs=[pl.BlockSpec(memory_space=pl.ANY)] * 3,
        out_specs=pl.BlockSpec(memory_space=pltpu.VMEM),
        scratch_shapes=[
            pltpu.VMEM((2, rows, columns), f32),
            pltpu.VMEM((levels, 2, rows, depth), f32),
            pltpu.VMEM((2, inv_rows, 2 * depth), f32),
            pltpu.VMEM((2 * inv_rows, 2 * depth), bf16),
            pltpu.VMEM((2 * inv_rows, 2 * depth), bf16),
            pltpu.VMEM((levels, 2 * rows, depth), bf16),
            pltpu.VMEM((levels, 2 * rows, depth), bf16),
            pltpu.VMEM((levels + 1, rows, columns), f32),
            pltpu.VMEM((2, rows, columns), f32),
            pltpu.VMEM((inv_rows, columns), f32),
            pltpu.VMEM((levels, depth // 2, columns), f32),
            pltpu.VMEM((rows, columns), f32),
            dma((levels + 2,)),
            dma((levels + 3,)),
            dma((levels + 3,)),
            dma((2 * nodes * levels,)),
            dma((2, PARTS)),
            dma((levels, levels + nodes)),
            dma((levels, nodes // 2, PARTS)),
        ],
        compiler_params=pltpu.CompilerParams(
            has_side_effects=True, vmem_limit_bytes=48 * 1024 * 1024
        ),
        cost_estimate=pl.CostEstimate(
            flops=2 * 6 * (2 * rows * depth * columns * levels),
            bytes_accessed=4 * (spikes.size + inverses.size + 2 * right_side.size),
            transcendentals=0,
        ),
    )(right_side, spikes, inverses)


def solution(mesh):
    in_specs = (P(("dom", "row"), None), P(None, ("dom", "row"), None), P("dom", "row", None))
    out_specs = P(("dom", "row"), None)
    return jax.shard_map(body, mesh=mesh, in_specs=in_specs, out_specs=out_specs, check_vma=False)
```

```python
import functools

import jax
import jax.numpy as jnp
from jax import lax
from jax.experimental import pallas as pl
from jax.experimental.pallas import tpu as pltpu
from jax.sharding import PartitionSpec as P

PARTS = 8
VMEM_LIMIT = 63 * 1024 * 1024 + 896 * 1024


def split_pair(value):
    high = value.astype(jnp.bfloat16)
    low = (value - high.astype(jnp.float32)).astype(jnp.bfloat16)
    return high, low


def bf_dot(left, right):
    return jnp.dot(left, right, preferred_element_type=jnp.float32)


def kernel(
    row_count,
    right_ref,
    spikes_ref,
    inverse_ref,
    out_ref,
    right_buf,
    spike_buf,
    inverse_buf,
    inv_hi,
    inv_lo,
    spk_hi,
    spk_lo,
    cur,
    tips,
    piece,
    halves,
    last,
    local_sem,
    pair_send,
    pair_recv,
    a_send,
    a_recv,
    b_send,
    b_recv,
):
    levels, rows, depth = spikes_ref.shape
    columns = right_ref.shape[1]
    half_columns = columns // 2
    inv_rows = inverse_ref.shape[1]
    nodes = row_count // 2
    half_nodes = nodes // 2
    dom = lax.axis_index("dom")
    row = lax.axis_index("row")
    core = lax.rem(row, 2)
    node = row // 2
    other = 1 - core
    lane = lax.broadcasted_iota(jnp.int32, (1, columns), 1)

    def place(dom_at, node_at):
        return {"dom": dom_at, "row": 2 * node_at + core}

    sibling = {"dom": dom, "row": 2 * node + other}

    def position(level):
        group = 1 << level
        offset = lax.rem(dom, 2 * group)
        is_left = offset < group
        if group >= 2:
            flipped = (group // 2 - 1 - offset // 2) * 2 + lax.rem(offset, 2)
            relative = jnp.where(is_left, flipped, offset - group)
        else:
            relative = offset - offset
        holder = jnp.where(is_left, node >= half_nodes, node < half_nodes)
        return group, offset, dom - offset, is_left, relative, holder

    def tree_dom(group, base, is_left, relative):
        if group >= 2:
            left = (group // 2 - 1 - relative // 2) * 2 + lax.rem(relative, 2)
        else:
            left = relative
        return base + jnp.where(is_left, left, group + relative)

    barrier = pltpu.get_barrier_semaphore()

    def greet(where):
        pl.semaphore_signal(barrier, inc=1, device_id=where)

    expected = nodes + 0 * dom
    greet(sibling)
    for step in range(1, nodes):
        greet(place(dom, lax.rem(node + step, nodes)))
    dom_count = lax.axis_size("dom")

    @pl.when((node == nodes - 1) & (dom > 0))
    def _():
        greet(place(dom - 1, nodes - 1))

    def count(condition):
        return jnp.where(condition, 1, 0)

    expected += count((node == nodes - 1) & (dom < dom_count - 1))
    for level in range(levels):
        group, offset, base, is_left, relative, holder = position(level)

        @pl.when((offset == max(group - 2, 0)) & (node >= half_nodes))
        def _():
            greet(place(base + group, node))

        expected += count((offset == group) & (node >= half_nodes))
        bit = group // 2
        while bit >= 1:
            @pl.when(holder & (lax.rem(relative, 2 * bit) == bit))
            def _(bit=bit):
                greet(place(tree_dom(group, base, is_left, relative - bit), node))

            expected += count(holder & (lax.rem(relative, 2 * bit) == 0))
            bit //= 2
    pl.semaphore_wait(barrier, expected)

    loads = [
        (right_ref, right_buf.at[core]),
        (inverse_ref.at[0], inverse_buf.at[core]),
    ] + [(spikes_ref.at[l], spike_buf.at[l, core]) for l in range(levels)]
    own, pair = [], []
    for index, (source, target) in enumerate(loads):
        send = pltpu.make_async_remote_copy(
            src_ref=source,
            dst_ref=target,
            send_sem=pair_send.at[index],
            recv_sem=pair_recv.at[index],
            device_id=sibling,
        )
        send.start()
        pair.append(send)
        copy = pltpu.make_async_copy(source, target, local_sem.at[index])
        copy.start()
        own.append(copy)

    def loaded(index):
        own[index].wait()
        pair[index].wait_recv()

    own_lanes = (lane < half_columns) == (core == 0)
    loaded(0)
    cur[0] = jnp.where(
        own_lanes, right_buf[core], pltpu.roll(right_buf[other], half_columns, 1)
    )

    def copy_to(source, target, send_sem, recv_sem, where):
        return pltpu.make_async_remote_copy(
            src_ref=source,
            dst_ref=target,
            send_sem=send_sem,
            recv_sem=recv_sem,
            device_id=where,
        )

    tip_chunk = rows // PARTS
    piece_chunk = inv_rows // PARTS
    tip_cut = [pl.ds(c * tip_chunk, tip_chunk) for c in range(PARTS)]
    piece_cut = [pl.ds(c * piece_chunk, piece_chunk) for c in range(PARTS)]
    waits = []

    def send_tips(source, slot, sem_at, c, where):
        copy_to(
            source.at[tip_cut[c]],
            tips.at[slot, tip_cut[c]],
            a_send.at[sem_at],
            a_recv.at[slot, c],
            where,
        ).start()

    def wait_tips(slot, c):
        copy_to(
            tips.at[slot, tip_cut[c]],
            tips.at[slot, tip_cut[c]],
            a_send.at[0],
            a_recv.at[slot, c],
            sibling,
        ).wait_recv()

    def packed(left, right):
        half = left.shape[0] // 2
        low = lane < half_columns
        straight = jnp.where(low, left[:half], right[half:])
        crossed = jnp.where(low, left[half:], right[:half])
        return straight + pltpu.roll(crossed, half_columns, 1)

    def product(hi_ref, lo_ref, messages):
        left = right = None
        for at, message in messages:
            high, low = split_pair(message)
            both = jnp.concatenate([high, low], axis=1)
            sums = []
            for side in range(2):
                cut = slice(at + side * rows, at + (side + 1) * rows)
                wide = bf_dot(hi_ref[:, cut], both)
                thin = bf_dot(lo_ref[:, cut], high)
                sums.append(wide[:, :columns] + (wide[:, columns:] + thin))
            left = sums[0] if left is None else left + sums[0]
            right = sums[1] if right is None else right + sums[1]
        return packed(left, right)

    def run_level(level):
        group, offset, base, is_left, relative, holder = position(level)
        is_solver = offset == group
        entry = max(group - 2, 0)
        from_bottom = (offset == group - 1) & (node == nodes - 1)

        @pl.when(from_bottom)
        def _():
            for c in range(PARTS):
                send_tips(cur.at[level], 0, 2 * nodes * level, c, place(dom + 1, nodes - 1))

        def across(step):
            return lax.rem(node + step, nodes)

        @pl.when(is_solver & (node == 0))
        def _():
            for c in range(PARTS):
                for step in range(1, nodes):
                    send_tips(cur.at[level], 1, 2 * nodes * level + step, c, place(dom, step))

        if level == 0:
            loaded(1)
            for side in range(2):
                high, low = split_pair(inverse_buf[side])
                at = slice(side * inv_rows, (side + 1) * inv_rows)
                inv_hi[at], inv_lo[at] = high, low

        piece_at = lax.rem(node, half_nodes)

        def spread(source, c, wait):
            def go(copy):
                copy.wait_send() if wait else copy.start()

            cut = piece_cut[c]
            target = halves.at[level, pl.ds(piece_at * inv_rows + c * piece_chunk, piece_chunk)]
            if wait:
                source, target = source, halves.at[level, pl.ds(piece_at * inv_rows, inv_rows)]
            else:
                source = source.at[cut]
            recv = b_recv.at[level, piece_at, c]
            bit, number = group // 2, 0
            while bit >= 1:
                child = relative + bit
                child_dom = tree_dom(group, base, is_left, child)

                @pl.when(lax.rem(relative, 2 * bit) == 0)
                def _(number=number, child_dom=child_dom):
                    go(copy_to(source, target, b_send.at[level, number], recv, place(child_dom, node)))

                bit //= 2
                number += 1
            for step in range(1, nodes):
                go(
                    copy_to(
                        source,
                        target,
                        b_send.at[level, levels + step],
                        recv,
                        place(dom, across(step)),
                    )
                )

        def to_left(c, wait):
            whole = pl.ds(piece_at * inv_rows, inv_rows)
            part = pl.ds(piece_at * inv_rows + c * piece_chunk, piece_chunk)
            copy = copy_to(
                piece if wait else piece.at[piece_cut[c]],
                halves.at[level, whole if wait else part],
                b_send.at[level, levels],
                b_recv.at[level, piece_at, c],
                place(base + entry, node),
            )
            copy.wait_send() if wait else copy.start()

        @pl.when(is_solver)
        def _():
            for c in range(PARTS):
                wait_tips(0, c)

                @pl.when(node == nodes - 1)
                def _():
                    for step in range(nodes - 1):
                        send_tips(
                            tips.at[0], 0, 2 * nodes * level + nodes + step, c, place(dom, step)
                        )

            @pl.when(node == 0)
            def _():
                tips[1] = cur[level]

            @pl.when(node != 0)
            def _():
                for c in range(PARTS):
                    wait_tips(1, c)

            piece[...] = product(inv_hi, inv_lo, [(0, tips[0]), (depth, tips[1])])

            @pl.when(node < half_nodes)
            def _():
                for c in range(PARTS):
                    spread(piece, c, False)
                halves[level, pl.ds(piece_at * inv_rows, inv_rows)] = piece[...]

            @pl.when(node >= half_nodes)
            def _():
                for c in range(PARTS):
                    to_left(c, False)

        loaded(2 + level)
        for side in range(2):
            high, low = split_pair(spike_buf[level, side])
            at = slice(side * rows, (side + 1) * rows)
            for value, target in ((high, spk_hi), (low, spk_lo)):
                if half_nodes > 1:
                    blocks = [
                        value[:, (2 * i + part) * inv_rows : (2 * i + part + 1) * inv_rows]
                        for part in range(2)
                        for i in range(half_nodes)
                    ]
                    value = jnp.concatenate(blocks, axis=1)
                target[level, at] = value

        for c in range(PARTS):
            for index in range(half_nodes):
                mine = is_solver & (node == index)
                forward = holder & (piece_at == index) & ~mine

                @pl.when(~mine)
                def _():
                    part = halves.at[level, pl.ds(index * inv_rows + c * piece_chunk, piece_chunk)]
                    copy_to(
                        part, part, b_send.at[0, 0], b_recv.at[level, index, c], sibling
                    ).wait_recv()

                @pl.when(forward)
                def _():
                    spread(halves.at[level, pl.ds(index * inv_rows, inv_rows)], c, False)

        update = product(spk_hi.at[level], spk_lo.at[level], [(0, halves[level])])
        cur[level + 1] = cur[level] - update

        def finish():
            @pl.when(from_bottom)
            def _():
                copy_to(
                    cur.at[level], tips.at[0], a_send.at[2 * nodes * level], a_recv.at[0, 0],
                    place(dom + 1, nodes - 1),
                ).wait_send()

            @pl.when(is_solver & (node == 0))
            def _():
                for step in range(1, nodes):
                    copy_to(
                        cur.at[level], tips.at[1], a_send.at[2 * nodes * level + step],
                        a_recv.at[1, 0], place(dom, step),
                    ).wait_send()

            @pl.when(is_solver & (node == nodes - 1))
            def _():
                for step in range(nodes - 1):
                    copy_to(
                        tips.at[0], tips.at[0], a_send.at[2 * nodes * level + nodes + step],
                        a_recv.at[0, 0], place(dom, step),
                    ).wait_send()

            @pl.when(is_solver & (node >= half_nodes))
            def _():
                to_left(0, True)

            @pl.when(holder)
            def _():
                spread(halves.at[level, pl.ds(piece_at * inv_rows, inv_rows)], 0, True)

        waits.append(finish)

    for level in range(levels):
        run_level(level)

    swap = copy_to(cur.at[levels], last, pair_send.at[levels + 2], pair_recv.at[levels + 2], sibling)
    swap.start()
    for finish in waits:
        finish()
    for send in pair:
        send.wait_send()
    swap.wait()
    out_ref[...] = jnp.where(own_lanes, cur[levels], pltpu.roll(last[...], half_columns, 1))


def body(right_side, spikes, inverses):
    row_count = lax.axis_size("row")
    rows, columns = right_side.shape
    levels, _, depth = spikes.shape
    inv_rows = inverses.shape[1]
    nodes = row_count // 2
    f32, bf16 = jnp.float32, jnp.bfloat16
    dma = pltpu.SemaphoreType.DMA
    return pl.pallas_call(
        functools.partial(kernel, row_count),
        out_shape=jax.ShapeDtypeStruct((rows, columns), f32),
        in_specs=[pl.BlockSpec(memory_space=pl.ANY)] * 3,
        out_specs=pl.BlockSpec(memory_space=pltpu.VMEM),
        scratch_shapes=[
            pltpu.VMEM((2, rows, columns), f32),
            pltpu.VMEM((levels, 2, rows, depth), f32),
            pltpu.VMEM((2, inv_rows, 2 * depth), f32),
            pltpu.VMEM((2 * inv_rows, 2 * depth), bf16),
            pltpu.VMEM((2 * inv_rows, 2 * depth), bf16),
            pltpu.VMEM((levels, 2 * rows, depth), bf16),
            pltpu.VMEM((levels, 2 * rows, depth), bf16),
            pltpu.VMEM((levels + 1, rows, columns), f32),
            pltpu.VMEM((2, rows, columns), f32),
            pltpu.VMEM((inv_rows, columns), f32),
            pltpu.VMEM((levels, depth // 2, columns), f32),
            pltpu.VMEM((rows, columns), f32),
            dma((levels + 2,)),
            dma((levels + 3,)),
            dma((levels + 3,)),
            dma((2 * nodes * levels,)),
            dma((2, PARTS)),
            dma((levels, levels + nodes)),
            dma((levels, nodes // 2, PARTS)),
        ],
        compiler_params=pltpu.CompilerParams(
            has_side_effects=True, vmem_limit_bytes=VMEM_LIMIT, collective_id=0
        ),
        cost_estimate=pl.CostEstimate(
            flops=2 * 6 * (2 * rows * depth * columns * levels),
            bytes_accessed=4 * (spikes.size + inverses.size + 2 * right_side.size),
            transcendentals=0,
        ),
    )(right_side, spikes, inverses)


def solution(mesh):
    in_specs = (P(("dom", "row"), None), P(None, ("dom", "row"), None), P("dom", "row", None))
    out_specs = P(("dom", "row"), None)
    return jax.shard_map(body, mesh=mesh, in_specs=in_specs, out_specs=out_specs, check_vma=False)
```

```python
import functools

import jax
import jax.numpy as jnp
from jax import lax
from jax.experimental import pallas as pl
from jax.experimental.pallas import tpu as pltpu
from jax.sharding import PartitionSpec as P

PARTS = 8
VMEM_LIMIT = 63 * 1024 * 1024 + 896 * 1024


def split_pair(value):
    high = value.astype(jnp.bfloat16)
    low = (value - high.astype(jnp.float32)).astype(jnp.bfloat16)
    return high, low


def bf_dot(left, right):
    return jnp.dot(left, right, preferred_element_type=jnp.float32)


def kernel(
    row_count,
    right_ref,
    spikes_ref,
    inverse_ref,
    out_ref,
    right_buf,
    spike_buf,
    inverse_buf,
    inv_hi,
    inv_lo,
    spk_hi,
    spk_lo,
    cur,
    tips,
    piece,
    halves,
    last,
    local_sem,
    pair_send,
    pair_recv,
    a_send,
    a_recv,
    b_send,
    b_recv,
    relay,
    relay_recv,
):
    levels, rows, depth = spikes_ref.shape
    columns = right_ref.shape[1]
    half_columns = columns // 2
    inv_rows = inverse_ref.shape[1]
    nodes = row_count // 2
    half_nodes = nodes // 2
    dom = lax.axis_index("dom")
    row = lax.axis_index("row")
    core = lax.rem(row, 2)
    node = row // 2
    other = 1 - core
    lane = lax.broadcasted_iota(jnp.int32, (1, columns), 1)

    def place(dom_at, node_at):
        return {"dom": dom_at, "row": 2 * node_at + core}

    sibling = {"dom": dom, "row": 2 * node + other}

    def position(level):
        group = 1 << level
        offset = lax.rem(dom, 2 * group)
        is_left = offset < group
        if group >= 2:
            flipped = (group // 2 - 1 - offset // 2) * 2 + lax.rem(offset, 2)
            relative = jnp.where(is_left, flipped, offset - group)
        else:
            relative = offset - offset
        holder = jnp.where(is_left, node >= half_nodes, node < half_nodes)
        return group, offset, dom - offset, is_left, relative, holder

    def tree_dom(group, base, is_left, relative):
        if group >= 2:
            left = (group // 2 - 1 - relative // 2) * 2 + lax.rem(relative, 2)
        else:
            left = relative
        return base + jnp.where(is_left, left, group + relative)

    barrier = pltpu.get_barrier_semaphore()

    def greet(where):
        pl.semaphore_signal(barrier, inc=1, device_id=where)

    expected = nodes + 0 * dom
    greet(sibling)
    for step in range(1, nodes):
        greet(place(dom, lax.rem(node + step, nodes)))
    dom_count = lax.axis_size("dom")

    @pl.when((node == nodes - 1) & (dom > 0))
    def _():
        greet(place(dom - 1, nodes - 1))

    def count(condition):
        return jnp.where(condition, 1, 0)

    expected += count((node == nodes - 1) & (dom < dom_count - 1))
    for level in range(levels):
        group, offset, base, is_left, relative, holder = position(level)

        @pl.when(offset == max(group - 2, 0))
        def _():
            greet(place(base + group, node))

        expected += count(offset == group)
        bit = group // 2
        while bit >= 1:
            @pl.when(lax.rem(relative, 2 * bit) == bit)
            def _(bit=bit):
                greet(place(tree_dom(group, base, is_left, relative - bit), node))

            expected += count(lax.rem(relative, 2 * bit) == 0)
            bit //= 2
    pl.semaphore_wait(barrier, expected)

    loads = [
        (right_ref, right_buf.at[core]),
        (inverse_ref.at[0], inverse_buf.at[core]),
    ] + [(spikes_ref.at[l], spike_buf.at[l, core]) for l in range(levels)]
    own, pair = [], []
    for index, (source, target) in enumerate(loads):
        send = pltpu.make_async_remote_copy(
            src_ref=source,
            dst_ref=target,
            send_sem=pair_send.at[index],
            recv_sem=pair_recv.at[index],
            device_id=sibling,
        )
        send.start()
        pair.append(send)
        copy = pltpu.make_async_copy(source, target, local_sem.at[index])
        copy.start()
        own.append(copy)

    def loaded(index):
        own[index].wait()
        pair[index].wait_recv()

    own_lanes = (lane < half_columns) == (core == 0)
    loaded(0)
    cur[0] = jnp.where(
        own_lanes, right_buf[core], pltpu.roll(right_buf[other], half_columns, 1)
    )

    def copy_to(source, target, send_sem, recv_sem, where):
        return pltpu.make_async_remote_copy(
            src_ref=source,
            dst_ref=target,
            send_sem=send_sem,
            recv_sem=recv_sem,
            device_id=where,
        )

    tip_chunk = rows // PARTS
    piece_chunk = inv_rows // PARTS
    tip_cut = [pl.ds(c * tip_chunk, tip_chunk) for c in range(PARTS)]
    piece_cut = [pl.ds(c * piece_chunk, piece_chunk) for c in range(PARTS)]
    waits = []

    def send_tips(source, slot, sem_at, c, where):
        copy_to(
            source.at[tip_cut[c]],
            tips.at[slot, tip_cut[c]],
            a_send.at[sem_at],
            a_recv.at[slot, c],
            where,
        ).start()

    def wait_tips(slot, c):
        copy_to(
            tips.at[slot, tip_cut[c]],
            tips.at[slot, tip_cut[c]],
            a_send.at[0],
            a_recv.at[slot, c],
            sibling,
        ).wait_recv()

    def packed(left, right):
        half = left.shape[0] // 2
        low = lane < half_columns
        straight = jnp.where(low, left[:half], right[half:])
        crossed = jnp.where(low, left[half:], right[:half])
        return straight + pltpu.roll(crossed, half_columns, 1)

    def product(hi_ref, lo_ref, messages):
        left = right = None
        for at, message in messages:
            high, low = split_pair(message)
            both = jnp.concatenate([high, low], axis=1)
            sums = []
            for side in range(2):
                cut = slice(at + side * rows, at + (side + 1) * rows)
                wide = bf_dot(hi_ref[:, cut], both)
                thin = bf_dot(lo_ref[:, cut], high)
                sums.append(wide[:, :columns] + (wide[:, columns:] + thin))
            left = sums[0] if left is None else left + sums[0]
            right = sums[1] if right is None else right + sums[1]
        return packed(left, right)

    def run_level(level):
        group, offset, base, is_left, relative, holder = position(level)
        is_solver = offset == group
        entry = max(group - 2, 0)
        from_bottom = (offset == group - 1) & (node == nodes - 1)

        @pl.when(from_bottom)
        def _():
            for c in range(PARTS):
                first = nodes - 1
                send_tips(
                    cur.at[level], 0, 2 * nodes * (levels + c % 2) + level, c, place(dom + 1, first)
                )

        def across(step):
            return lax.rem(node + step, nodes)

        @pl.when(is_solver & (node == 0))
        def _():
            for c in range(PARTS):
                for step in range(1, nodes):
                    send_tips(cur.at[level], 1, 2 * nodes * level + step, c, place(dom, step))

        if level == 0:
            loaded(1)
            for side in range(2):
                high, low = split_pair(inverse_buf[side])
                at = slice(side * inv_rows, (side + 1) * inv_rows)
                inv_hi[at], inv_lo[at] = high, low

        piece_at = lax.rem(node, half_nodes)

        def slot(c):
            return halves.at[level, pl.ds(piece_at * inv_rows + c * piece_chunk, piece_chunk)]

        def some(share):
            return halves.at[level, pl.ds(0, inv_rows // share)]

        def down(source, c, share=0):
            bit, number = group // 2, 0
            while bit >= 1:

                @pl.when(lax.rem(relative, 2 * bit) == 0)
                def _(number=number, bit=bit):
                    where = place(tree_dom(group, base, is_left, relative + bit), node)
                    sem = b_send.at[level, number]
                    if share:
                        copy_to(some(share), some(share), sem, b_recv.at[level, 0, 0], where).wait_send()
                    else:
                        recv = b_recv.at[level, piece_at, c]
                        copy_to(source.at[piece_cut[c]], slot(c), sem, recv, where).start()

                bit //= 2
                number += 1

        def aside(source, c, share=0):
            for step in range(1, nodes):
                where = place(dom, across(step))
                sem = b_send.at[level, levels + 1 + step]
                if share:
                    copy_to(some(share), some(share), sem, b_recv.at[level, 0, 0], where).wait_send()
                else:
                    recv = b_recv.at[level, piece_at, c]
                    copy_to(source.at[piece_cut[c]], slot(c), sem, recv, where).start()

        def to_left(c, share=0):
            where = place(base + entry, node)
            sem = b_send.at[level, levels + c % 2]
            if share:
                copy_to(some(share), some(share), sem, b_recv.at[level, 0, 0], where).wait_send()
            else:
                recv = b_recv.at[level, piece_at, c]
                source = piece if c % 2 == 0 else relay
                copy_to(source.at[piece_cut[c]], slot(c), sem, recv, where).start()

        def to_relay(c, share=0):
            where = place(dom, piece_at)
            sem = b_send.at[level, levels + 1]
            if share:
                copy_to(some(share), some(share), sem, relay_recv.at[0], where).wait_send()
            else:
                cut = piece_cut[c]
                copy_to(piece.at[cut], relay.at[cut], sem, relay_recv.at[c], where).start()

        @pl.when(is_solver)
        def _():
            for c in range(PARTS):
                wait_tips(0, c)

                @pl.when(node == nodes - 1)
                def _():
                    for step in range(1, nodes):
                        send_tips(
                            tips.at[0],
                            0,
                            2 * nodes * level + nodes + step,
                            c,
                            place(dom, across(step)),
                        )

            @pl.when(node == 0)
            def _():
                tips[1] = cur[level]

            @pl.when(node != 0)
            def _():
                for c in range(PARTS):
                    wait_tips(1, c)

            piece[...] = product(inv_hi, inv_lo, [(0, tips[0]), (depth, tips[1])])

            @pl.when(node < half_nodes)
            def _():
                for c in range(PARTS):
                    if c % 2 == 0:
                        down(piece, c)
                    aside(piece, c)
                halves[level, pl.ds(piece_at * inv_rows, inv_rows)] = piece[...]
                for c in range(1, PARTS, 2):
                    part = relay.at[piece_cut[c]]
                    copy_to(part, part, b_send.at[0, 0], relay_recv.at[c], sibling).wait_recv()
                    to_left(c)

            @pl.when(node >= half_nodes)
            def _():
                for c in range(PARTS):
                    to_left(c) if c % 2 == 0 else to_relay(c)

        loaded(2 + level)
        for side in range(2):
            high, low = split_pair(spike_buf[level, side])
            at = slice(side * rows, (side + 1) * rows)
            for value, target in ((high, spk_hi), (low, spk_lo)):
                if half_nodes > 1:
                    blocks = [
                        value[:, (2 * i + part) * inv_rows : (2 * i + part + 1) * inv_rows]
                        for part in range(2)
                        for i in range(half_nodes)
                    ]
                    value = jnp.concatenate(blocks, axis=1)
                target[level, at] = value

        for c in range(PARTS):
            for index in range(half_nodes):
                mine = is_solver & (node == index)
                turn = holder if c % 2 == 0 else ~holder
                forward = turn & (piece_at == index) & ~mine

                @pl.when(~mine)
                def _():
                    part = halves.at[level, pl.ds(index * inv_rows + c * piece_chunk, piece_chunk)]
                    copy_to(
                        part, part, b_send.at[0, 0], b_recv.at[level, index, c], sibling
                    ).wait_recv()

                @pl.when(forward)
                def _():
                    source = halves.at[level, pl.ds(index * inv_rows, inv_rows)]
                    down(source, c)

                    @pl.when(~is_solver)
                    def _():
                        aside(source, c)

        update = product(spk_hi.at[level], spk_lo.at[level], [(0, halves[level])])
        cur[level + 1] = cur[level] - update

        def finish():
            half_tips = tips.at[0, pl.ds(0, rows // 2)]

            def sent(ref, index):
                copy_to(ref, ref, a_send.at[index], a_recv.at[0, 0], sibling).wait_send()

            @pl.when(from_bottom)
            def _():
                for part in range(2):
                    sent(half_tips, 2 * nodes * (levels + part) + level)

            @pl.when(is_solver & (node == 0))
            def _():
                for step in range(1, nodes):
                    sent(tips.at[1], 2 * nodes * level + step)

            @pl.when(is_solver & (node == nodes - 1))
            def _():
                for step in range(1, nodes):
                    sent(tips.at[0], 2 * nodes * level + nodes + step)

            @pl.when(is_solver & (node >= half_nodes))
            def _():
                to_left(0, 2)
                to_relay(1, 2)

            down(piece, 0, 2)

            @pl.when(is_solver & (node < half_nodes))
            def _():
                aside(piece, 0, 1)
                to_left(1, 2)

            @pl.when(~is_solver)
            def _():
                aside(piece, 0, 2)

        waits.append(finish)

    for level in range(levels):
        run_level(level)

    swap = copy_to(cur.at[levels], last, pair_send.at[levels + 2], pair_recv.at[levels + 2], sibling)
    swap.start()
    for finish in waits:
        finish()
    for send in pair:
        send.wait_send()
    swap.wait()
    out_ref[...] = jnp.where(own_lanes, cur[levels], pltpu.roll(last[...], half_columns, 1))


def body(right_side, spikes, inverses):
    row_count = lax.axis_size("row")
    rows, columns = right_side.shape
    levels, _, depth = spikes.shape
    inv_rows = inverses.shape[1]
    nodes = row_count // 2
    f32, bf16 = jnp.float32, jnp.bfloat16
    dma = pltpu.SemaphoreType.DMA
    return pl.pallas_call(
        functools.partial(kernel, row_count),
        out_shape=jax.ShapeDtypeStruct((rows, columns), f32),
        in_specs=[pl.BlockSpec(memory_space=pl.ANY)] * 3,
        out_specs=pl.BlockSpec(memory_space=pltpu.VMEM),
        scratch_shapes=[
            pltpu.VMEM((2, rows, columns), f32),
            pltpu.VMEM((levels, 2, rows, depth), f32),
            pltpu.VMEM((2, inv_rows, 2 * depth), f32),
            pltpu.VMEM((2 * inv_rows, 2 * depth), bf16),
            pltpu.VMEM((2 * inv_rows, 2 * depth), bf16),
            pltpu.VMEM((levels, 2 * rows, depth), bf16),
            pltpu.VMEM((levels, 2 * rows, depth), bf16),
            pltpu.VMEM((levels + 1, rows, columns), f32),
            pltpu.VMEM((2, rows, columns), f32),
            pltpu.VMEM((inv_rows, columns), f32),
            pltpu.VMEM((levels, depth // 2, columns), f32),
            pltpu.VMEM((rows, columns), f32),
            dma((levels + 2,)),
            dma((levels + 3,)),
            dma((levels + 3,)),
            dma((2 * nodes * (levels + 2),)),
            dma((2, PARTS)),
            dma((levels, levels + 1 + nodes)),
            dma((levels, nodes // 2, PARTS)),
            pltpu.VMEM((inv_rows, columns), f32),
            dma((PARTS,)),
        ],
        compiler_params=pltpu.CompilerParams(
            has_side_effects=True, vmem_limit_bytes=VMEM_LIMIT, collective_id=0
        ),
        cost_estimate=pl.CostEstimate(
            flops=2 * 6 * (2 * rows * depth * columns * levels),
            bytes_accessed=4 * (spikes.size + inverses.size + 2 * right_side.size),
            transcendentals=0,
        ),
    )(right_side, spikes, inverses)


def solution(mesh):
    in_specs = (P(("dom", "row"), None), P(None, ("dom", "row"), None), P("dom", "row", None))
    out_specs = P(("dom", "row"), None)
    return jax.shard_map(body, mesh=mesh, in_specs=in_specs, out_specs=out_specs, check_vma=False)
```
